32 devices in a mesh: groups: 2 (over y), seq: 16 (over z, x, core).
Axes of the slice: x: 2, y: 2, z: 4, core: 2. Of those that a mesh axis runs over, the one named last changes fastest.
Arguments:
- tokens: bfloat16 [16384, 768], P(('groups', 'seq')), parts along dimension 0, may hold values from -6 to 6
- weight: bfloat16 [768, 3, 768], P('seq'), may hold values from -0.125 to 0.125
- cotangent: bfloat16 [16384, 768], P(('groups', 'seq')), parts along dimension 0, may hold values from -6 to 6
Outputs:
- output: bfloat16 [16384, 768], P(('groups', 'seq')), parts along dimension 0
- d_tokens: bfloat16 [16384, 768], P(('groups', 'seq')), parts along dimension 0
- d_weight: float32 [1536, 3, 768], P(('groups', 'seq')), parts along dimension 0
The draws below stay inside these ranges and needn't reach their ends.
There are 2 independent parts, one for each index of `groups`. The reference program is written for one: setup_inputs(seed, part) draws one part's arguments, and reference() takes and returns one part's arrays. A program takes and returns all parts, laid end to end along the dimension named above; an argument that names none is the same for every part. Nothing has to cross between parts.
All inputs are finite; a program needn't handle non-finite values.
Results may differ from the reference program's by a relative error of at most 0.0054.
Values may be sent and summed in bfloat16 or wider, within the bound.
A program may use at most 64 MiB of HBM per device.

```python
import jax
import jax.numpy as jnp
from jax import lax

C = 768
TOKEN_COUNT = 8192
DILATION_SPAN = 1024


def spiked(array, key, source, target, shards_of, factor):
    def block_of(position):
        return (jnp.arange(array.shape[position]) // (array.shape[position] // shards_of)).reshape((-1,) + (1,) * (array.ndim - 1 - position))

    first = jax.random.permutation(key, shards_of)[block_of(target)]
    far = (block_of(target) + shards_of // 2) % shards_of
    return jnp.where((block_of(source) == first) | (block_of(source) == far), factor * array, array)


def shard_levels(stream_key, extent, shards, smallest, high):
    gain = 1.0
    for axis_at, shards_of in shards:
        draws = jax.random.uniform(jax.random.fold_in(jax.random.fold_in(stream_key, 6), axis_at), (shards_of,), jnp.float32, smallest / len(shards), high / len(shards))
        gain = gain * jnp.repeat(jnp.exp(draws), extent[axis_at] // shards_of).reshape((-1,) + (1,) * (len(extent) - 1 - axis_at))
    return gain


def scatter_about(rng, dims, spread, most, cuts=(), held_as=jnp.bfloat16):
    entries = spread * jax.random.normal(rng, dims, jnp.float32)
    if cuts:
        entries = entries * shard_levels(rng, dims, cuts, -0.22, 0.18)
    return jnp.clip(entries, -most, most).astype(held_as)


def gaussian_with(stream_key, shape, scale, reach, shards, heavy, held_as=jnp.bfloat16):
    values = scale * jax.random.normal(stream_key, shape, jnp.float32)
    if shards:
        values = values * shard_levels(stream_key, shape, shards, -0.22, 0.18)
    return jnp.clip(spiked(values, jax.random.fold_in(stream_key, 3), *heavy), -reach, reach).astype(held_as)


def setup_inputs(seed: int = 0, part: int = 0) -> dict:
    keys = jax.random.split(jax.random.key(seed), 4)
    own_keys = jax.random.split(jax.random.fold_in(keys[3], part), 4)
    return {
        "tokens": scatter_about(own_keys[0], (TOKEN_COUNT, C), 1.0, 6.0, ((0, 16),)),
        "weight": scatter_about(keys[1], (C, 3, C), (3 * C) ** -0.5, 0.125, ((0, 16),)),
        "cotangent": gaussian_with(own_keys[2], (TOKEN_COUNT, C), 1.0, 6.0, ((0, 16),), (0, 1, 16, 2.0)),
    }


def displace_rows(values, offset):
    if offset > 0:
        return jnp.pad(values, ((offset, 0), (0, 0)))[:values.shape[0]]
    return jnp.pad(values, ((0, -offset), (0, 0)))[-offset:]

def reference(tokens, weight, cotangent):
    x = tokens.astype(jnp.float32)
    inv = lax.rsqrt(lax.optimization_barrier(jnp.mean(x * x, axis=1, keepdims=True)) + 1e-06)
    normalized_rows = (x * inv).astype(jnp.bfloat16)
    filter_taps = jnp.concatenate([displace_rows(normalized_rows, DILATION_SPAN), normalized_rows, displace_rows(normalized_rows, -DILATION_SPAN)], axis=1)
    flat = weight.reshape(C, 3 * C)
    pre = lax.dot_general(filter_taps, flat, (((1,), (1,)), ((), ())), preferred_element_type=jnp.float32)
    output = (x + jax.nn.gelu(pre)).astype(jnp.bfloat16)
    slope = jax.jvp(jax.nn.gelu, (pre,), (jnp.ones_like(pre),))[1]
    grad_out = cotangent.astype(jnp.float32)
    preactivation_gradient = (grad_out * slope).astype(jnp.bfloat16)
    normalized_gradient = jnp.dot(displace_rows(preactivation_gradient, -DILATION_SPAN), weight[:, 0, :], preferred_element_type=jnp.float32)
    normalized_gradient = normalized_gradient + jnp.dot(preactivation_gradient, weight[:, 1, :], preferred_element_type=jnp.float32)
    normalized_gradient = normalized_gradient + jnp.dot(displace_rows(preactivation_gradient, DILATION_SPAN), weight[:, 2, :], preferred_element_type=jnp.float32)
    inner = lax.optimization_barrier(jnp.mean(normalized_gradient * x, axis=1, keepdims=True))
    d_tokens = (grad_out + inv * normalized_gradient - x * inv * inv * inv * inner).astype(jnp.bfloat16)
    term = lax.dot_general(preactivation_gradient, filter_taps, (((0,), (0,)), ((), ())), preferred_element_type=jnp.float32)
    d_weight = (term / jnp.sqrt(jnp.float32(TOKEN_COUNT))).reshape(C, 3, C)
    return (output, d_tokens, d_weight)
```

```python
import functools
import math

import jax
import jax.numpy as jnp
from jax import lax
from jax.experimental import pallas as pl
from jax.experimental.pallas import tpu as pltpu
from jax.sharding import PartitionSpec as P

SPAN = 2
MESH = pl.DeviceIdType.MESH
F32 = jnp.float32
BF16 = jnp.bfloat16

T_TOK, T_COT, T_UP, T_DOWN, T_SIDE, T_Z, T_Y, T_CORE = 0, 1, 2, 3, 4, 5, 8, 11
T_OUT, T_DTOK, T_PUP, T_PDOWN, T_RC, T_RX, T_RZ, T_COUNT = 19, 20, 21, 24, 27, 30, 33, 42


def kernel(
    scale, tok_ref, w_ref, cot_ref, out_ref, dtok_ref, dw_ref,
    xs, gs, taps, grads, weights, gt, gtp, sums, core_send, core_recv,
    x_send, x_recv, z_sum, z_send, z_recv, outs, dtoks, send_sem, recv_sem,
):
    rows, width = tok_ref.shape
    half = rows // 2
    shard = w_ref.shape[0]
    y = lax.axis_index("groups")
    s = lax.axis_index("seq")
    z, x, c = s // 4, (s // 2) % 2, s % 2
    px = (y, s + 2 - 4 * x)
    pc = (y, s + 1 - 2 * c)
    py = (1 - y, s)
    pz = {j: (y, ((z + j) % 4) * 4 + 2 * x + c) for j in (1, 2, 3)}
    up = pz[1]
    down = pz[3]

    barrier = pltpu.get_barrier_semaphore()
    for peer in (px, pc, py, pz[1], pz[2], pz[3]):
        pl.semaphore_signal(barrier, inc=1, device_id=peer, device_id_type=MESH)
    pl.semaphore_wait(barrier, 6)

    def remote(t, src, dst, peer):
        return pltpu.make_async_remote_copy(
            src_ref=src, dst_ref=dst, send_sem=send_sem.at[t], recv_sem=recv_sem.at[t],
            device_id=peer, device_id_type=MESH,
        )

    def block(ref, index, size):
        return ref.at[pl.ds(pl.multiple_of(index * size, size), size)]

    def w_copy(t, index, peer):
        place = block(weights, index, shard)
        return remote(t, place, place, peer)

    tok_copy = remote(T_TOK, block(tok_ref, 1 - x, half), xs.at[x], px)
    cot_copy = remote(T_COT, block(cot_ref, 1 - x, half), gs.at[x], px)
    weights[pl.ds(pl.multiple_of(s * shard, shard), shard), :] = w_ref[...]
    other_x = s + 2 - 4 * x
    carried = z * 4 + 2 * y + c

    def start_z():
        for j in (1, 2, 3):
            w_copy(T_Z + j - 1, carried, pz[j]).start()

    @pl.when(x == y)
    def _():
        w_copy(T_SIDE, s, px).start()
        start_z()

    tok_copy.start()
    w_copy(T_CORE, s, pc).start()

    up_copy = remote(T_UP, taps.at[pl.ds(2 * half, half)], taps.at[pl.ds(0, half)], up)
    down_copy = remote(T_DOWN, taps.at[pl.ds(half, half)], taps.at[pl.ds(3 * half, half)], down)

    def normalize(slot):
        value = xs[slot].astype(F32)
        inv = lax.rsqrt(jnp.mean(value * value, axis=1, keepdims=True) + 1e-06)
        start = pl.multiple_of((slot + 1) * half, half)
        taps[pl.ds(start, half), :] = (value * inv).astype(BF16)

        @pl.when((slot == 0) & (z > 0))
        def _():
            down_copy.start()

        @pl.when((slot == 1) & (z < 3))
        def _():
            up_copy.start()

    xs[x] = tok_ref[pl.ds(pl.multiple_of(x * half, half), half), :]
    gs[x] = cot_ref[pl.ds(pl.multiple_of(x * half, half), half), :]
    normalize(x)

    @pl.when(x != y)
    def _():
        w_copy(T_SIDE, other_x, px).wait_recv()
        start_z()
        w_copy(T_SIDE, other_x, py).start()

    tok_copy.wait_recv()
    normalize(1 - x)
    cot_copy.start()

    @pl.when(z == 0)
    def _():
        taps[0:half, :] = jnp.zeros((half, width), BF16)
        grads[0:half, :] = jnp.zeros((half, width), BF16)

    @pl.when(z == 3)
    def _():
        taps[3 * half :, :] = jnp.zeros((half, width), BF16)
        grads[3 * half :, :] = jnp.zeros((half, width), BF16)

    @pl.when(x == y)
    def _():
        w_copy(T_SIDE, other_x, py).wait_recv()

    w_copy(T_CORE + 1, other_x, pc).start()
    for j in (1, 3, 2):
        index = ((z + 4 - j) % 4) * 4 + 2 * y + c
        w_copy(T_Z + j - 1, index, pz[j]).wait_recv()
        w_copy(T_Y + j - 1, index, py).start()
        w_copy(T_CORE + 1 + j, index, pc).start()
    for j in (1, 3, 2):
        index = ((z + 4 - j) % 4) * 4 + 2 * (1 - y) + c
        w_copy(T_Y + j - 1, index, py).wait_recv()
        w_copy(T_CORE + 4 + j, index, pc).start()
    across = 1 - c
    own_core = [z * 4 + 2 * x, z * 4 + 2 * (1 - x)]
    own_core += [((z + 4 - j) % 4) * 4 + 2 * y for j in (1, 2, 3)]
    own_core += [((z + 4 - j) % 4) * 4 + 2 * (1 - y) for j in (1, 2, 3)]
    for q, index in enumerate(own_core):
        w_copy(T_CORE + q, index + across, pc).wait_recv()

    @pl.when(z > 0)
    def _():
        up_copy.wait_recv()

    @pl.when(z < 3)
    def _():
        down_copy.wait_recv()

    cot_copy.wait_recv()

    part = width // 3
    root = math.sqrt(2.0 / math.pi)

    def pup(n):
        cols = pl.ds(pl.multiple_of(n * part, part), part)
        return remote(
            T_PUP + n, grads.at[pl.ds(2 * half, half), cols], grads.at[pl.ds(0, half), cols], up
        )

    def pdown(n):
        cols = pl.ds(pl.multiple_of(n * part, part), part)
        return remote(
            T_PDOWN + n, grads.at[pl.ds(half, half), cols], grads.at[pl.ds(3 * half, half), cols], down
        )

    @pl.loop(0, 3)
    def _(n):
        cols = pl.ds(pl.multiple_of(n * part, part), part)
        pre = jnp.zeros((rows, part), F32)
        for k in range(3):
            pre = pre + lax.dot_general(
                taps[k * half : k * half + rows, :],
                weights[cols, k * width : (k + 1) * width],
                (((1,), (1,)), ((), ())),
                preferred_element_type=F32,
            )
        square = pre * pre
        bend = jnp.tanh(root * pre * (1.0 + 0.044715 * square))
        cdf = 0.5 * (1.0 + bend)
        slope = cdf + 0.5 * pre * (1.0 - bend * bend) * (root * (1.0 + 3 * 0.044715 * square))
        value = xs[:, :, cols].reshape(rows, part).astype(F32)
        grad = gs[:, :, cols].reshape(rows, part).astype(F32)
        outs[:, :, cols] = (value + pre * cdf).astype(BF16).reshape(2, half, part)
        d_pre = grad * slope
        grads[half : 3 * half, cols] = d_pre.astype(BF16)

        @pl.when(z < 3)
        def _():
            pup(n).start()

        @pl.when(z > 0)
        def _():
            pdown(n).start()

        gt[cols, :] = d_pre.T.astype(BF16)

    out_copy = remote(T_OUT, outs.at[1 - x], block(out_ref, x, half), px)
    out_copy.start()
    for source in range(16):
        place = (source % 2) * 8 + ((source // 2) % 2) * 4 + source // 4
        gtp[place * shard : (place + 1) * shard, :] = gt[source * shard : (source + 1) * shard, :]
    out_ref[pl.ds(pl.multiple_of(x * half, half), half), :] = outs[x]

    most = 8 * shard

    def core_copy(k):
        return remote(T_RC + k, core_send.at[k], core_recv.at[k], pc)

    def x_copy(k):
        return remote(T_RX + k, x_send.at[k], x_recv.at[k], px)

    def z_copy(k, j):
        there = block(z_send.at[k], (z + j) % 4, shard)
        return remote(T_RZ + 3 * k + j - 1, there, z_recv.at[k, j - 1], pz[j])

    def weight_term(k):
        right = taps[k * half : k * half + rows, :]
        there = gtp[pl.ds(pl.multiple_of((1 - c) * most, most), most), :]
        core_send[k] = jnp.dot(there, right, preferred_element_type=F32).astype(BF16)
        core_copy(k).start()
        here = gtp[pl.ds(pl.multiple_of(c * most, most), most), :]
        sums[k] = jnp.dot(here, right, preferred_element_type=F32)

    def over_core(k):
        core_copy(k).wait_recv()
        there = pl.ds(pl.multiple_of((1 - x) * 4 * shard, 4 * shard), 4 * shard)
        x_send[k] = (sums[k, there, :] + core_recv[k, there, :].astype(F32)).astype(BF16)
        x_copy(k).start()

    def over_x(k):
        x_copy(k).wait_recv()
        here = pl.ds(pl.multiple_of(x * 4 * shard, 4 * shard), 4 * shard)
        total = sums[k, here, :] + core_recv[k, here, :].astype(F32) + x_recv[k].astype(F32)
        z_sum[k] = total
        z_send[k] = total.astype(BF16)
        for j in (1, 2, 3):
            z_copy(k, j).start()

    def over_z(k):
        total = z_sum[k, pl.ds(pl.multiple_of(z * shard, shard), shard), :]
        for j in (1, 2, 3):
            z_copy(k, j).wait_recv()
            total = total + z_recv[k, j - 1].astype(F32)
        dw_ref[:, k * width : (k + 1) * width] = total * scale

    def input_gradient(slot):
        total = jnp.zeros((half, width), F32)
        for k in range(3):
            left = grads[pl.ds(pl.multiple_of((slot + 2 - k) * half, half), half), :]
            total = total + jnp.dot(
                left, weights[:, k * width : (k + 1) * width], preferred_element_type=F32
            )
        value = xs[slot].astype(F32)
        inv = lax.rsqrt(jnp.mean(value * value, axis=1, keepdims=True) + 1e-06)
        inner = jnp.mean(total * value, axis=1, keepdims=True)
        grad = gs[slot].astype(F32)
        dtoks[slot] = (grad + inv * total - value * inv * inv * inv * inner).astype(BF16)

    dtok_copy = remote(T_DTOK, dtoks.at[1 - x], block(dtok_ref, x, half), px)
    weight_term(0)
    weight_term(1)
    over_core(0)
    weight_term(2)
    over_core(1)
    over_core(2)

    @pl.when(z > 0)
    def _():
        for n in range(3):
            pup(n).wait_recv()

    @pl.when(z < 3)
    def _():
        for n in range(3):
            pdown(n).wait_recv()

    input_gradient(1 - x)
    dtok_copy.start()
    over_x(0)
    input_gradient(x)
    dtok_ref[pl.ds(pl.multiple_of(x * half, half), half), :] = dtoks[x]
    over_x(1)
    over_x(2)
    over_z(0)
    over_z(1)
    over_z(2)

    out_copy.wait_recv()
    dtok_copy.wait_recv()

    for copy in (tok_copy, cot_copy, out_copy, dtok_copy):
        copy.wait_send()

    @pl.when(z > 0)
    def _():
        down_copy.wait_send()
        for n in range(3):
            pdown(n).wait_send()

    @pl.when(z < 3)
    def _():
        up_copy.wait_send()
        for n in range(3):
            pup(n).wait_send()

    for t in [T_SIDE] + [T_Z + j for j in range(3)] + [T_Y + j for j in range(3)]:
        w_copy(t, s, px).wait_send()
    for q in range(8):
        w_copy(T_CORE + q, s, pc).wait_send()
    for k in range(3):
        core_copy(k).wait_send()
        x_copy(k).wait_send()
        for j in (1, 2, 3):
            z_copy(k, j).wait_send()


def fused(tokens, weight, cotangent):
    rows, width = tokens.shape
    shard = weight.shape[0]
    half = rows // 2
    scale = 1.0 / math.sqrt(rows * lax.axis_size("seq"))
    vmem = pl.BlockSpec(memory_space=pltpu.VMEM)
    output, d_tokens, d_weight = pl.pallas_call(
        functools.partial(kernel, scale),
        out_shape=(
            jax.ShapeDtypeStruct((rows, width), BF16),
            jax.ShapeDtypeStruct((rows, width), BF16),
            jax.ShapeDtypeStruct((shard, 3 * width), F32),
        ),
        in_specs=[vmem] * 3,
        out_specs=(vmem, vmem, vmem),
        scratch_shapes=[
            pltpu.VMEM((2, half, width), BF16),
            pltpu.VMEM((2, half, width), BF16),
            pltpu.VMEM((4 * half, width), BF16),
            pltpu.VMEM((4 * half, width), BF16),
            pltpu.VMEM((width, 3 * width), BF16),
            pltpu.VMEM((width, rows), BF16),
            pltpu.VMEM((width, rows), BF16),
            pltpu.VMEM((3, 8 * shard, width), F32),
            pltpu.VMEM((3, 8 * shard, width), BF16),
            pltpu.VMEM((3, 8 * shard, width), BF16),
            pltpu.VMEM((3, 4 * shard, width), BF16),
            pltpu.VMEM((3, 4 * shard, width), BF16),
            pltpu.VMEM((3, 4 * shard, width), F32),
            pltpu.VMEM((3, 4 * shard, width), BF16),
            pltpu.VMEM((3, 3, shard, width), BF16),
            pltpu.VMEM((2, half, width), BF16),
            pltpu.VMEM((2, half, width), BF16),
            pltpu.SemaphoreType.DMA((T_COUNT,)),
            pltpu.SemaphoreType.DMA((T_COUNT,)),
        ],
        compiler_params=pltpu.CompilerParams(
            collective_id=0, has_side_effects=True, vmem_limit_bytes=52 * 1024 * 1024
        ),
        cost_estimate=pl.CostEstimate(
            flops=6 * rows * 3 * width * width, bytes_accessed=6 * rows * width * 2, transcendentals=rows * width
        ),
    )(tokens, weight.reshape(shard, 3 * width), cotangent)
    return output, d_tokens, d_weight.reshape(shard, 3, width)


def shifted(value, axis, steps):
    count = lax.axis_size(axis)
    first, last = (max(0, -steps), min(count, count - steps))
    return lax.ppermute(value, axis, [(source, source + steps) for source in range(first, last)])


def from_lower(values):
    return shifted(values, "seq", SPAN)


def received_upper(values):
    return shifted(values, "seq", -SPAN)


def general(tokens, weight, cotangent):
    rows = tokens.shape[0]
    width = tokens.shape[1]
    seq_count = lax.axis_size("seq")
    x = tokens.astype(jnp.float32)
    inv = lax.rsqrt(jnp.mean(x * x, axis=1, keepdims=True) + 1e-06)
    normalized_rows = (x * inv).astype(jnp.bfloat16)
    filter_taps = jnp.concatenate(
        [from_lower(normalized_rows), normalized_rows, received_upper(normalized_rows)], axis=1
    )
    full_weight = lax.all_gather(weight, "seq", axis=0, tiled=True)
    pre = lax.dot_general(
        filter_taps,
        full_weight.reshape(width, 3 * width),
        (((1,), (1,)), ((), ())),
        preferred_element_type=jnp.float32,
    )
    output = (x + jax.nn.gelu(pre)).astype(jnp.bfloat16)
    slope = jax.jvp(jax.nn.gelu, (pre,), (jnp.ones_like(pre),))[1]
    grad_out = cotangent.astype(jnp.float32)
    preactivation_gradient = (grad_out * slope).astype(jnp.bfloat16)
    normalized_gradient = jnp.dot(
        received_upper(preactivation_gradient),
        full_weight[:, 0, :],
        preferred_element_type=jnp.float32,
    )
    normalized_gradient = normalized_gradient + jnp.dot(
        preactivation_gradient, full_weight[:, 1, :], preferred_element_type=jnp.float32
    )
    normalized_gradient = normalized_gradient + jnp.dot(
        from_lower(preactivation_gradient), full_weight[:, 2, :], preferred_element_type=jnp.float32
    )
    inner = jnp.mean(normalized_gradient * x, axis=1, keepdims=True)
    d_tokens = (grad_out + inv * normalized_gradient - x * inv * inv * inv * inner).astype(
        jnp.bfloat16
    )
    term = lax.dot_general(
        preactivation_gradient,
        filter_taps,
        (((0,), (0,)), ((), ())),
        preferred_element_type=jnp.float32,
    )
    owned = lax.psum_scatter(term, "seq", scatter_dimension=0, tiled=True)
    scale_factor = 1.0 / jnp.sqrt(jnp.float32(rows * seq_count))
    d_weight = (owned * scale_factor).reshape(owned.shape[0], 3, width)
    return (output, d_tokens, d_weight)


def solution(mesh):
    placed = (P(("groups", "seq"), None), P("seq", None, None), P(("groups", "seq"), None))
    small = mesh.shape["groups"] == 2 and mesh.shape["seq"] == 16
    return jax.shard_map(
        fused if small else general,
        mesh=mesh,
        in_specs=placed,
        out_specs=(
            P(("groups", "seq"), None),
            P(("groups", "seq"), None),
            P(("groups", "seq"), None, None),
        ),
        check_vma=False,
    )
```

```python
import functools
import math

import jax
import jax.numpy as jnp
from jax import lax
from jax.experimental import pallas as pl
from jax.experimental.pallas import tpu as pltpu
from jax.sharding import PartitionSpec as P

SPAN = 2
MESH = pl.DeviceIdType.MESH
F32 = jnp.float32
BF16 = jnp.bfloat16

T_TOK, T_COT, T_UP, T_DOWN, T_SIDE, T_CORE = 0, 1, 2, 3, 4, 6
T_ZUP, T_ZDOWN, T_YUP, T_YDOWN = 14, 20, 26, 32
T_OUT, T_DTOK, T_PUP, T_PDOWN, T_RC, T_RX, T_RZ, T_COUNT = 38, 40, 41, 43, 45, 48, 51, 60


def kernel(
    scale, tok_ref, w_ref, cot_ref, out_ref, dtok_ref, dw_ref,
    xs, gs, taps, grads, weights, gt, gtp, sums, core_send, core_recv,
    x_send, x_recv, z_sum, z_send, z_recv, outs, dtoks, send_sem, recv_sem,
):
    rows, width = tok_ref.shape
    half = rows // 2
    shard = w_ref.shape[0]
    y = lax.axis_index("groups")
    s = lax.axis_index("seq")
    z, x, c = s // 4, (s // 2) % 2, s % 2
    px = (y, s + 2 - 4 * x)
    pc = (y, s + 1 - 2 * c)
    py = (1 - y, s)
    pz = {j: (y, ((z + j) % 4) * 4 + 2 * x + c) for j in (1, 2, 3)}
    up = pz[1]
    down = pz[3]

    barrier = pltpu.get_barrier_semaphore()
    for peer in (px, pc, py, pz[1], pz[2], pz[3]):
        pl.semaphore_signal(barrier, inc=1, device_id=peer, device_id_type=MESH)
    pl.semaphore_wait(barrier, 6)

    def remote(t, src, dst, peer):
        return pltpu.make_async_remote_copy(
            src_ref=src, dst_ref=dst, send_sem=send_sem.at[t], recv_sem=recv_sem.at[t],
            device_id=peer, device_id_type=MESH,
        )

    def block(ref, index, size):
        return ref.at[pl.ds(pl.multiple_of(index * size, size), size)]

    def w_copy(t, index, peer):
        place = block(weights, index, shard)
        return remote(t, place, place, peer)

    most_cols = weights.shape[1] // 2

    def half_copy(t, index, side, peer):
        place = weights.at[
            pl.ds(pl.multiple_of(index * shard, shard), shard),
            pl.ds(pl.multiple_of(side * most_cols, most_cols), most_cols),
        ]
        return remote(t, place, place, peer)

    def at(d, q):
        return (z + d) * 4 + (2 * x + c if q == 0 else 2 * (1 - x) + c)

    def send_z(d, q):
        @pl.when((z < 3) & (z - d >= 0))
        def _():
            half_copy(T_ZUP + 2 * d + q, at(-d, q), y, up).start()

        @pl.when((z > 0) & (z + d <= 3))
        def _():
            half_copy(T_ZDOWN + 2 * d + q, at(d, q), y, down).start()

    def take_z(d, q):
        @pl.when(z - 1 - d >= 0)
        def _():
            half_copy(T_ZUP + 2 * d + q, at(-1 - d, q), y, up).wait_recv()
            half_copy(T_YUP + 2 * d + q, at(-1 - d, q), y, py).start()

        @pl.when(z + 1 + d <= 3)
        def _():
            half_copy(T_ZDOWN + 2 * d + q, at(1 + d, q), y, down).wait_recv()
            half_copy(T_YDOWN + 2 * d + q, at(1 + d, q), y, py).start()

        if d < 2:
            send_z(d + 1, q)

    def take_y(d, q):
        @pl.when(z - 1 - d >= 0)
        def _():
            half_copy(T_YUP + 2 * d + q, at(-1 - d, q), 1 - y, py).wait_recv()
            w_copy(T_CORE + 2 + 2 * (2 - d) + q, at(-1 - d, q), pc).start()

        @pl.when(z + 1 + d <= 3)
        def _():
            half_copy(T_YDOWN + 2 * d + q, at(1 + d, q), 1 - y, py).wait_recv()
            w_copy(T_CORE + 2 + 2 * d + q, at(1 + d, q), pc).start()

    tok_copy = remote(T_TOK, block(tok_ref, 1 - x, half), xs.at[x], px)
    cot_copy = remote(T_COT, block(cot_ref, 1 - x, half), gs.at[x], px)
    weights[pl.ds(pl.multiple_of(s * shard, shard), shard), :] = w_ref[...]
    other_x = s + 2 - 4 * x
    half_copy(T_SIDE, s, y, px).start()
    send_z(0, 0)
    half_copy(T_SIDE + 1, s, 1 - y, px).start()
    tok_copy.start()
    w_copy(T_CORE, s, pc).start()

    up_copy = remote(T_UP, taps.at[pl.ds(2 * half, half)], taps.at[pl.ds(0, half)], up)
    down_copy = remote(T_DOWN, taps.at[pl.ds(half, half)], taps.at[pl.ds(3 * half, half)], down)

    def normalize(slot):
        value = xs[slot].astype(F32)
        inv = lax.rsqrt(jnp.mean(value * value, axis=1, keepdims=True) + 1e-06)
        start = pl.multiple_of((slot + 1) * half, half)
        taps[pl.ds(start, half), :] = (value * inv).astype(BF16)

        @pl.when((slot == 0) & (z > 0))
        def _():
            down_copy.start()

        @pl.when((slot == 1) & (z < 3))
        def _():
            up_copy.start()

    xs[x] = tok_ref[pl.ds(pl.multiple_of(x * half, half), half), :]
    gs[x] = cot_ref[pl.ds(pl.multiple_of(x * half, half), half), :]
    half_copy(T_SIDE, other_x, y, px).wait_recv()
    send_z(0, 1)
    normalize(x)

    @pl.when(z == 0)
    def _():
        taps[0:half, :] = jnp.zeros((half, width), BF16)
        grads[0:half, :] = jnp.zeros((half, width), BF16)

    @pl.when(z == 3)
    def _():
        taps[3 * half :, :] = jnp.zeros((half, width), BF16)
        grads[3 * half :, :] = jnp.zeros((half, width), BF16)

    take_z(0, 0)
    half_copy(T_SIDE + 1, other_x, 1 - y, px).wait_recv()
    w_copy(T_CORE + 1, other_x, pc).start()
    take_z(0, 1)
    tok_copy.wait_recv()
    cot_copy.start()
    normalize(1 - x)
    take_z(1, 0)
    take_y(0, 0)
    take_z(1, 1)
    take_y(0, 1)

    part = width // 2
    root = math.sqrt(2.0 / math.pi)

    def pup(n):
        cols = pl.ds(pl.multiple_of(n * part, part), part)
        return remote(
            T_PUP + n, grads.at[pl.ds(2 * half, half), cols], grads.at[pl.ds(0, half), cols], up
        )

    def pdown(n):
        cols = pl.ds(pl.multiple_of(n * part, part), part)
        return remote(
            T_PDOWN + n, grads.at[pl.ds(half, half), cols], grads.at[pl.ds(3 * half, half), cols], down
        )

    def out_copy(n):
        cols = pl.ds(pl.multiple_of(n * part, part), part)
        there = out_ref.at[pl.ds(pl.multiple_of(x * half, half), half), cols]
        return remote(T_OUT + n, outs.at[1 - x, :, cols], there, px)

    def forward(n):
        cols = pl.ds(pl.multiple_of(n * part, part), part)
        pre = jnp.zeros((rows, part), F32)
        for k in range(3):
            pre = pre + lax.dot_general(
                taps[k * half : k * half + rows, :],
                weights[cols, k * width : (k + 1) * width],
                (((1,), (1,)), ((), ())),
                preferred_element_type=F32,
            )
        square = pre * pre
        bend = jnp.tanh(root * pre * (1.0 + 0.044715 * square))
        cdf = 0.5 * (1.0 + bend)
        slope = cdf + 0.5 * pre * (1.0 - bend * bend) * (root * (1.0 + 3 * 0.044715 * square))
        value = xs[:, :, cols].reshape(rows, part).astype(F32)
        grad = gs[:, :, cols].reshape(rows, part).astype(F32)
        outs[:, :, cols] = (value + pre * cdf).astype(BF16).reshape(2, half, part)
        out_copy(n).start()
        d_pre = grad * slope
        grads[half : 3 * half, cols] = d_pre.astype(BF16)

        @pl.when(z < 3)
        def _():
            pup(n).start()

        @pl.when(z > 0)
        def _():
            pdown(n).start()

        gt[cols, :] = d_pre.T.astype(BF16)

    def core_arrival(q, index):
        w_copy(T_CORE + q, index + 1 - 2 * c, pc).wait_recv()

    def layer_arrival(d):
        for q in (0, 1):
            core_arrival(2 + 2 * (d - 1) + q, ((z + d) % 4) * 4 + (2 * x if q == 0 else 2 * (1 - x)) + c)

    near = z // 2

    @pl.when(z > 0)
    def _():
        up_copy.wait_recv()

    @pl.when(z < 3)
    def _():
        down_copy.wait_recv()

    cot_copy.wait_recv()
    core_arrival(0, s)
    core_arrival(1, other_x)

    @pl.when(z % 2 == 0)
    def _():
        layer_arrival(1)

    @pl.when(z % 2 == 1)
    def _():
        layer_arrival(3)

    @pl.loop(0, 2)
    def _(turn):
        @pl.when(turn == 1)
        def _():
            for q in (0, 1):
                take_z(2, q)
                take_y(1, q)
            for q in (0, 1):
                take_y(2, q)
            layer_arrival(2)

            @pl.when(z % 2 == 0)
            def _():
                layer_arrival(3)

            @pl.when(z % 2 == 1)
            def _():
                layer_arrival(1)

        forward(near + turn - 2 * near * turn)

    for source in range(16):
        place = (source % 2) * 8 + ((source // 2) % 2) * 4 + source // 4
        gtp[place * shard : (place + 1) * shard, :] = gt[source * shard : (source + 1) * shard, :]
    out_ref[pl.ds(pl.multiple_of(x * half, half), half), :] = outs[x]

    most = 8 * shard

    def core_copy(k):
        return remote(T_RC + k, core_send.at[k], core_recv.at[k], pc)

    def x_copy(k):
        return remote(T_RX + k, x_send.at[k], x_recv.at[k], px)

    def z_copy(k, j):
        there = block(z_send.at[k], (z + j) % 4, shard)
        return remote(T_RZ + 3 * k + j - 1, there, z_recv.at[k, j - 1], pz[j])

    def weight_term(k):
        right = taps[k * half : k * half + rows, :]
        there = gtp[pl.ds(pl.multiple_of((1 - c) * most, most), most), :]
        core_send[k] = jnp.dot(there, right, preferred_element_type=F32).astype(BF16)
        core_copy(k).start()
        here = gtp[pl.ds(pl.multiple_of(c * most, most), most), :]
        sums[k] = jnp.dot(here, right, preferred_element_type=F32)

    def over_core(k):
        core_copy(k).wait_recv()
        there = pl.ds(pl.multiple_of((1 - x) * 4 * shard, 4 * shard), 4 * shard)
        x_send[k] = (sums[k, there, :] + core_recv[k, there, :].astype(F32)).astype(BF16)
        x_copy(k).start()

    def over_x(k):
        x_copy(k).wait_recv()
        here = pl.ds(pl.multiple_of(x * 4 * shard, 4 * shard), 4 * shard)
        total = sums[k, here, :] + core_recv[k, here, :].astype(F32) + x_recv[k].astype(F32)
        z_sum[k] = total
        z_send[k] = total.astype(BF16)
        for j in (1, 2, 3):
            z_copy(k, j).start()

    def over_z(k):
        total = z_sum[k, pl.ds(pl.multiple_of(z * shard, shard), shard), :]
        for j in (1, 2, 3):
            z_copy(k, j).wait_recv()
            total = total + z_recv[k, j - 1].astype(F32)
        dw_ref[:, k * width : (k + 1) * width] = total * scale

    def input_gradient(slot):
        total = jnp.zeros((half, width), F32)
        for k in range(3):
            left = grads[pl.ds(pl.multiple_of((slot + 2 - k) * half, half), half), :]
            total = total + jnp.dot(
                left, weights[:, k * width : (k + 1) * width], preferred_element_type=F32
            )
        value = xs[slot].astype(F32)
        inv = lax.rsqrt(jnp.mean(value * value, axis=1, keepdims=True) + 1e-06)
        inner = jnp.mean(total * value, axis=1, keepdims=True)
        grad = gs[slot].astype(F32)
        dtoks[slot] = (grad + inv * total - value * inv * inv * inv * inner).astype(BF16)

    dtok_copy = remote(T_DTOK, dtoks.at[1 - x], block(dtok_ref, x, half), px)
    weight_term(0)
    weight_term(1)
    over_core(0)
    weight_term(2)
    over_core(1)
    over_core(2)

    @pl.when(z > 0)
    def _():
        for n in range(2):
            pup(n).wait_recv()

    @pl.when(z < 3)
    def _():
        for n in range(2):
            pdown(n).wait_recv()

    input_gradient(1 - x)
    dtok_copy.start()
    over_x(0)
    input_gradient(x)
    dtok_ref[pl.ds(pl.multiple_of(x * half, half), half), :] = dtoks[x]
    over_x(1)
    over_x(2)
    over_z(0)
    over_z(1)
    over_z(2)

    for n in range(2):
        out_copy(n).wait_recv()
        out_copy(n).wait_send()
    dtok_copy.wait_recv()

    for copy in (tok_copy, cot_copy, dtok_copy):
        copy.wait_send()

    @pl.when(z > 0)
    def _():
        down_copy.wait_send()
        for n in range(2):
            pdown(n).wait_send()

    @pl.when(z < 3)
    def _():
        up_copy.wait_send()
        for n in range(2):
            pup(n).wait_send()

    for t in (T_SIDE, T_SIDE + 1):
        half_copy(t, s, y, px).wait_send()
    for d in range(3):
        for q in (0, 1):

            @pl.when((z < 3) & (z - d >= 0))
            def _():
                half_copy(T_ZUP + 2 * d + q, s, y, up).wait_send()

            @pl.when((z > 0) & (z + d <= 3))
            def _():
                half_copy(T_ZDOWN + 2 * d + q, s, y, down).wait_send()

            @pl.when(z - 1 - d >= 0)
            def _():
                half_copy(T_YUP + 2 * d + q, s, y, py).wait_send()

            @pl.when(z + 1 + d <= 3)
            def _():
                half_copy(T_YDOWN + 2 * d + q, s, y, py).wait_send()

    for q in range(8):
        w_copy(T_CORE + q, s, pc).wait_send()
    for k in range(3):
        core_copy(k).wait_send()
        x_copy(k).wait_send()
        for j in (1, 2, 3):
            z_copy(k, j).wait_send()


def fused(tokens, weight, cotangent):
    rows, width = tokens.shape
    shard = weight.shape[0]
    half = rows // 2
    scale = 1.0 / math.sqrt(rows * lax.axis_size("seq"))
    vmem = pl.BlockSpec(memory_space=pltpu.VMEM)
    output, d_tokens, d_weight = pl.pallas_call(
        functools.partial(kernel, scale),
        out_shape=(
            jax.ShapeDtypeStruct((rows, width), BF16),
            jax.ShapeDtypeStruct((rows, width), BF16),
            jax.ShapeDtypeStruct((shard, 3 * width), F32),
        ),
        in_specs=[vmem] * 3,
        out_specs=(vmem, vmem, vmem),
        scratch_shapes=[
            pltpu.VMEM((2, half, width), BF16),
            pltpu.VMEM((2, half, width), BF16),
            pltpu.VMEM((4 * half, width), BF16),
            pltpu.VMEM((4 * half, width), BF16),
            pltpu.VMEM((width, 3 * width), BF16),
            pltpu.VMEM((width, rows), BF16),
            pltpu.VMEM((width, rows), BF16),
            pltpu.VMEM((3, 8 * shard, width), F32),
            pltpu.VMEM((3, 8 * shard, width), BF16),
            pltpu.VMEM((3, 8 * shard, width), BF16),
            pltpu.VMEM((3, 4 * shard, width), BF16),
            pltpu.VMEM((3, 4 * shard, width), BF16),
            pltpu.VMEM((3, 4 * shard, width), F32),
            pltpu.VMEM((3, 4 * shard, width), BF16),
            pltpu.VMEM((3, 3, shard, width), BF16),
            pltpu.VMEM((2, half, width), BF16),
            pltpu.VMEM((2, half, width), BF16),
            pltpu.SemaphoreType.DMA((T_COUNT,)),
            pltpu.SemaphoreType.DMA((T_COUNT,)),
        ],
        compiler_params=pltpu.CompilerParams(
            collective_id=0, has_side_effects=True, vmem_limit_bytes=52 * 1024 * 1024
        ),
        cost_estimate=pl.CostEstimate(
            flops=6 * rows * 3 * width * width, bytes_accessed=6 * rows * width * 2, transcendentals=rows * width
        ),
    )(tokens, weight.reshape(shard, 3 * width), cotangent)
    return output, d_tokens, d_weight.reshape(shard, 3, width)


def shifted(value, axis, steps):
    count = lax.axis_size(axis)
    first, last = (max(0, -steps), min(count, count - steps))
    return lax.ppermute(value, axis, [(source, source + steps) for source in range(first, last)])


def from_lower(values):
    return shifted(values, "seq", SPAN)


def received_upper(values):
    return shifted(values, "seq", -SPAN)


def general(tokens, weight, cotangent):
    rows = tokens.shape[0]
    width = tokens.shape[1]
    seq_count = lax.axis_size("seq")
    x = tokens.astype(jnp.float32)
    inv = lax.rsqrt(jnp.mean(x * x, axis=1, keepdims=True) + 1e-06)
    normalized_rows = (x * inv).astype(jnp.bfloat16)
    filter_taps = jnp.concatenate(
        [from_lower(normalized_rows), normalized_rows, received_upper(normalized_rows)], axis=1
    )
    full_weight = lax.all_gather(weight, "seq", axis=0, tiled=True)
    pre = lax.dot_general(
        filter_taps,
        full_weight.reshape(width, 3 * width),
        (((1,), (1,)), ((), ())),
        preferred_element_type=jnp.float32,
    )
    output = (x + jax.nn.gelu(pre)).astype(jnp.bfloat16)
    slope = jax.jvp(jax.nn.gelu, (pre,), (jnp.ones_like(pre),))[1]
    grad_out = cotangent.astype(jnp.float32)
    preactivation_gradient = (grad_out * slope).astype(jnp.bfloat16)
    normalized_gradient = jnp.dot(
        received_upper(preactivation_gradient),
        full_weight[:, 0, :],
        preferred_element_type=jnp.float32,
    )
    normalized_gradient = normalized_gradient + jnp.dot(
        preactivation_gradient, full_weight[:, 1, :], preferred_element_type=jnp.float32
    )
    normalized_gradient = normalized_gradient + jnp.dot(
        from_lower(preactivation_gradient), full_weight[:, 2, :], preferred_element_type=jnp.float32
    )
    inner = jnp.mean(normalized_gradient * x, axis=1, keepdims=True)
    d_tokens = (grad_out + inv * normalized_gradient - x * inv * inv * inv * inner).astype(
        jnp.bfloat16
    )
    term = lax.dot_general(
        preactivation_gradient,
        filter_taps,
        (((0,), (0,)), ((), ())),
        preferred_element_type=jnp.float32,
    )
    owned = lax.psum_scatter(term, "seq", scatter_dimension=0, tiled=True)
    scale_factor = 1.0 / jnp.sqrt(jnp.float32(rows * seq_count))
    d_weight = (owned * scale_factor).reshape(owned.shape[0], 3, width)
    return (output, d_tokens, d_weight)


def solution(mesh):
    placed = (P(("groups", "seq"), None), P("seq", None, None), P(("groups", "seq"), None))
    small = mesh.shape["groups"] == 2 and mesh.shape["seq"] == 16
    return jax.shard_map(
        fused if small else general,
        mesh=mesh,
        in_specs=placed,
        out_specs=(
            P(("groups", "seq"), None),
            P(("groups", "seq"), None),
            P(("groups", "seq"), None, None),
        ),
        check_vma=False,
    )
```

```python
import functools
import math

import jax
import jax.numpy as jnp
from jax import lax
from jax.experimental import pallas as pl
from jax.experimental.pallas import tpu as pltpu
from jax.sharding import PartitionSpec as P

SPAN = 2
MESH = pl.DeviceIdType.MESH
F32 = jnp.float32
BF16 = jnp.bfloat16

T_TOK, T_COT, T_UP, T_DOWN, T_SIDE, T_CORE = 0, 1, 2, 3, 4, 6
T_ZUP, T_ZDOWN, T_YUP, T_YDOWN = 14, 20, 26, 32
T_OUT, T_DTOK, T_PUP, T_PDOWN, T_RC, T_RX, T_RZ, T_COUNT = 38, 40, 41, 43, 45, 51, 57, 66


def kernel(
    scale, tok_ref, w_ref, cot_ref, out_ref, dtok_ref, dw_ref,
    xs, gs, taps, grads, weights, gtp, sums, core_send, core_recv,
    x_send, x_recv, z_sum, z_send, z_recv, outs, dtoks, send_sem, recv_sem,
):
    rows, width = tok_ref.shape
    half = rows // 2
    shard = w_ref.shape[0]
    y = lax.axis_index("groups")
    s = lax.axis_index("seq")
    z, x, c = s // 4, (s // 2) % 2, s % 2
    px = (y, s + 2 - 4 * x)
    pc = (y, s + 1 - 2 * c)
    py = (1 - y, s)
    pz = {j: (y, ((z + j) % 4) * 4 + 2 * x + c) for j in (1, 2, 3)}
    up = pz[1]
    down = pz[3]

    barrier = pltpu.get_barrier_semaphore()
    for peer in (px, pc, py, pz[1], pz[2], pz[3]):
        pl.semaphore_signal(barrier, inc=1, device_id=peer, device_id_type=MESH)
    pl.semaphore_wait(barrier, 6)

    def remote(t, src, dst, peer):
        return pltpu.make_async_remote_copy(
            src_ref=src, dst_ref=dst, send_sem=send_sem.at[t], recv_sem=recv_sem.at[t],
            device_id=peer, device_id_type=MESH,
        )

    def block(ref, index, size):
        return ref.at[pl.ds(pl.multiple_of(index * size, size), size)]

    def w_copy(t, index, peer):
        place = block(weights, index, shard)
        return remote(t, place, place, peer)

    most_cols = weights.shape[1] // 2

    def half_copy(t, index, side, peer):
        place = weights.at[
            pl.ds(pl.multiple_of(index * shard, shard), shard),
            pl.ds(pl.multiple_of(side * most_cols, most_cols), most_cols),
        ]
        return remote(t, place, place, peer)

    def at(d, q):
        return (z + d) * 4 + (2 * x + c if q == 0 else 2 * (1 - x) + c)

    def send_z(d, q):
        @pl.when((z < 3) & (z - d >= 0))
        def _():
            half_copy(T_ZUP + 2 * d + q, at(-d, q), y, up).start()

        @pl.when((z > 0) & (z + d <= 3))
        def _():
            half_copy(T_ZDOWN + 2 * d + q, at(d, q), y, down).start()

    def take_z(d, q):
        @pl.when(z - 1 - d >= 0)
        def _():
            half_copy(T_ZUP + 2 * d + q, at(-1 - d, q), y, up).wait_recv()
            half_copy(T_YUP + 2 * d + q, at(-1 - d, q), y, py).start()

        @pl.when(z + 1 + d <= 3)
        def _():
            half_copy(T_ZDOWN + 2 * d + q, at(1 + d, q), y, down).wait_recv()
            half_copy(T_YDOWN + 2 * d + q, at(1 + d, q), y, py).start()

        if d < 2:
            send_z(d + 1, q)

    def take_y(d, q):
        @pl.when(z - 1 - d >= 0)
        def _():
            half_copy(T_YUP + 2 * d + q, at(-1 - d, q), 1 - y, py).wait_recv()
            w_copy(T_CORE + 2 + 2 * (2 - d) + q, at(-1 - d, q), pc).start()

        @pl.when(z + 1 + d <= 3)
        def _():
            half_copy(T_YDOWN + 2 * d + q, at(1 + d, q), 1 - y, py).wait_recv()
            w_copy(T_CORE + 2 + 2 * d + q, at(1 + d, q), pc).start()

    tok_copy = remote(T_TOK, block(tok_ref, 1 - x, half), xs.at[x], px)
    cot_copy = remote(T_COT, block(cot_ref, 1 - x, half), gs.at[x], px)
    weights[pl.ds(pl.multiple_of(s * shard, shard), shard), :] = w_ref[...]
    other_x = s + 2 - 4 * x
    half_copy(T_SIDE, s, y, px).start()
    send_z(0, 0)
    half_copy(T_SIDE + 1, s, 1 - y, px).start()
    tok_copy.start()
    w_copy(T_CORE, s, pc).start()

    up_copy = remote(T_UP, taps.at[pl.ds(2 * half, half)], taps.at[pl.ds(0, half)], up)
    down_copy = remote(T_DOWN, taps.at[pl.ds(half, half)], taps.at[pl.ds(3 * half, half)], down)

    def normalize(slot):
        value = xs[slot].astype(F32)
        inv = lax.rsqrt(jnp.mean(value * value, axis=1, keepdims=True) + 1e-06)
        start = pl.multiple_of((slot + 1) * half, half)
        taps[pl.ds(start, half), :] = (value * inv).astype(BF16)

        @pl.when((slot == 0) & (z > 0))
        def _():
            down_copy.start()

        @pl.when((slot == 1) & (z < 3))
        def _():
            up_copy.start()

    xs[x] = tok_ref[pl.ds(pl.multiple_of(x * half, half), half), :]
    gs[x] = cot_ref[pl.ds(pl.multiple_of(x * half, half), half), :]
    half_copy(T_SIDE, other_x, y, px).wait_recv()
    send_z(0, 1)
    normalize(x)

    @pl.when(z == 0)
    def _():
        taps[0:half, :] = jnp.zeros((half, width), BF16)
        grads[0:half, :] = jnp.zeros((half, width), BF16)

    @pl.when(z == 3)
    def _():
        taps[3 * half :, :] = jnp.zeros((half, width), BF16)
        grads[3 * half :, :] = jnp.zeros((half, width), BF16)

    take_z(0, 0)
    half_copy(T_SIDE + 1, other_x, 1 - y, px).wait_recv()
    w_copy(T_CORE + 1, other_x, pc).start()
    take_z(0, 1)
    tok_copy.wait_recv()
    cot_copy.start()
    normalize(1 - x)
    take_z(1, 0)
    take_y(0, 0)
    take_z(1, 1)
    take_y(0, 1)

    part = width // 2
    root = math.sqrt(2.0 / math.pi)

    def pup(n):
        cols = pl.ds(pl.multiple_of(n * part, part), part)
        return remote(
            T_PUP + n, grads.at[pl.ds(2 * half, half), cols], grads.at[pl.ds(0, half), cols], up
        )

    def pdown(n):
        cols = pl.ds(pl.multiple_of(n * part, part), part)
        return remote(
            T_PDOWN + n, grads.at[pl.ds(half, half), cols], grads.at[pl.ds(3 * half, half), cols], down
        )

    def out_copy(n):
        cols = pl.ds(pl.multiple_of(n * part, part), part)
        there = out_ref.at[pl.ds(pl.multiple_of(x * half, half), half), cols]
        return remote(T_OUT + n, outs.at[1 - x, :, cols], there, px)

    def forward(n):
        cols = pl.ds(pl.multiple_of(n * part, part), part)
        pre = jnp.zeros((rows, part), F32)
        for k in range(3):
            pre = pre + lax.dot_general(
                taps[k * half : k * half + rows, :],
                weights[cols, k * width : (k + 1) * width],
                (((1,), (1,)), ((), ())),
                preferred_element_type=F32,
            )
        square = pre * pre
        bend = jnp.tanh(root * pre * (1.0 + 0.044715 * square))
        cdf = 0.5 * (1.0 + bend)
        slope = cdf + 0.5 * pre * (1.0 - bend * bend) * (root * (1.0 + 3 * 0.044715 * square))
        value = xs[:, :, cols].reshape(rows, part).astype(F32)
        grad = gs[:, :, cols].reshape(rows, part).astype(F32)
        outs[:, :, cols] = (value + pre * cdf).astype(BF16).reshape(2, half, part)
        out_copy(n).start()
        d_pre = grad * slope
        grads[half : 3 * half, cols] = d_pre.astype(BF16)

        @pl.when(z < 3)
        def _():
            pup(n).start()

        @pl.when(z > 0)
        def _():
            pdown(n).start()

        turned = d_pre.T.astype(BF16)
        for source in range(8):
            place = n * 8 + (source % 2) * 4 + ((source // 2) % 2) * 2 + source // 4
            gtp[pl.ds(pl.multiple_of(place * shard, shard), shard), :] = turned[
                source * shard : (source + 1) * shard
            ]

    def core_arrival(q, index):
        w_copy(T_CORE + q, index + 1 - 2 * c, pc).wait_recv()

    def layer_arrival(d):
        for q in (0, 1):
            core_arrival(2 + 2 * (d - 1) + q, ((z + d) % 4) * 4 + (2 * x if q == 0 else 2 * (1 - x)) + c)

    near = z // 2

    most = 4 * shard

    def core_copy(u):
        return remote(T_RC + u, core_send.at[u], core_recv.at[u], pc)

    def x_copy(u):
        return remote(T_RX + u, x_send.at[u], x_recv.at[u], px)

    def z_copy(u, layer):
        j = (layer - z + 4) % 4
        k = u % 3
        there = block(z_send.at[u], layer % 2, shard)
        return remote(
            T_RZ + 3 * k + j - 1, there, z_recv.at[k, j - 1], (y, layer * 4 + 2 * x + c)
        )

    def z_targets(u):
        if u < 3:
            return [near * 2 + 1 - z % 2]
        return [(1 - near) * 2, (1 - near) * 2 + 1]

    def weight_term(u):
        k = u % 3
        n = near if u < 3 else 1 - near
        right = taps[k * half : k * half + rows, :]
        there = gtp[pl.ds(pl.multiple_of((2 * n + 1 - c) * most, most), most), :]
        core_send[u] = jnp.dot(there, right, preferred_element_type=F32).astype(BF16)
        core_copy(u).start()
        here = gtp[pl.ds(pl.multiple_of((2 * n + c) * most, most), most), :]
        sums[u] = jnp.dot(here, right, preferred_element_type=F32)

    def over_core(u):
        core_copy(u).wait_recv()
        there = pl.ds(pl.multiple_of((1 - x) * 2 * shard, 2 * shard), 2 * shard)
        x_send[u] = (sums[u, there, :] + core_recv[u, there, :].astype(F32)).astype(BF16)
        x_copy(u).start()

    def over_x(u):
        x_copy(u).wait_recv()
        here = pl.ds(pl.multiple_of(x * 2 * shard, 2 * shard), 2 * shard)
        total = sums[u, here, :] + core_recv[u, here, :].astype(F32) + x_recv[u].astype(F32)
        if u < 3:
            z_sum[u] = total
        z_send[u] = total.astype(BF16)
        for layer in z_targets(u):
            z_copy(u, layer).start()

    def over_z(k):
        total = z_sum[k, pl.ds(pl.multiple_of((z % 2) * shard, shard), shard), :]
        for j in (1, 2, 3):
            remote(
                T_RZ + 3 * k + j - 1, block(z_send.at[k], 0, shard), z_recv.at[k, j - 1], pz[j]
            ).wait_recv()
            total = total + z_recv[k, j - 1].astype(F32)
        dw_ref[:, k * width : (k + 1) * width] = total * scale

    def input_gradient(slot):
        total = jnp.zeros((half, width), F32)
        for k in range(3):
            left = grads[pl.ds(pl.multiple_of((slot + 2 - k) * half, half), half), :]
            total = total + jnp.dot(
                left, weights[:, k * width : (k + 1) * width], preferred_element_type=F32
            )
        value = xs[slot].astype(F32)
        inv = lax.rsqrt(jnp.mean(value * value, axis=1, keepdims=True) + 1e-06)
        inner = jnp.mean(total * value, axis=1, keepdims=True)
        grad = gs[slot].astype(F32)
        dtoks[slot] = (grad + inv * total - value * inv * inv * inv * inner).astype(BF16)

    dtok_copy = remote(T_DTOK, dtoks.at[1 - x], block(dtok_ref, x, half), px)

    @pl.when(z > 0)
    def _():
        up_copy.wait_recv()

    @pl.when(z < 3)
    def _():
        down_copy.wait_recv()

    cot_copy.wait_recv()
    core_arrival(0, s)
    core_arrival(1, other_x)

    @pl.when(z % 2 == 0)
    def _():
        layer_arrival(1)

    @pl.when(z % 2 == 1)
    def _():
        layer_arrival(3)

    forward(near)
    weight_term(0)
    for q in (0, 1):
        take_z(2, q)
        take_y(1, q)
    weight_term(1)
    over_core(0)
    for q in (0, 1):
        take_y(2, q)
    weight_term(2)
    over_core(1)
    over_core(2)
    layer_arrival(2)

    @pl.when(z % 2 == 0)
    def _():
        layer_arrival(3)

    @pl.when(z % 2 == 1)
    def _():
        layer_arrival(1)

    forward(1 - near)
    weight_term(3)
    over_x(0)
    weight_term(4)
    over_core(3)
    over_x(1)
    weight_term(5)
    over_core(4)
    over_x(2)
    over_core(5)
    out_ref[pl.ds(pl.multiple_of(x * half, half), half), :] = outs[x]

    @pl.when(z > 0)
    def _():
        for n in range(2):
            pup(n).wait_recv()

    @pl.when(z < 3)
    def _():
        for n in range(2):
            pdown(n).wait_recv()

    input_gradient(1 - x)
    dtok_copy.start()
    over_x(3)
    input_gradient(x)
    dtok_ref[pl.ds(pl.multiple_of(x * half, half), half), :] = dtoks[x]
    over_x(4)
    over_x(5)
    over_z(0)
    over_z(1)
    over_z(2)

    for n in range(2):
        out_copy(n).wait_recv()
        out_copy(n).wait_send()
    dtok_copy.wait_recv()

    for copy in (tok_copy, cot_copy, dtok_copy):
        copy.wait_send()

    @pl.when(z > 0)
    def _():
        down_copy.wait_send()
        for n in range(2):
            pdown(n).wait_send()

    @pl.when(z < 3)
    def _():
        up_copy.wait_send()
        for n in range(2):
            pup(n).wait_send()

    for t in (T_SIDE, T_SIDE + 1):
        half_copy(t, s, y, px).wait_send()
    for d in range(3):
        for q in (0, 1):

            @pl.when((z < 3) & (z - d >= 0))
            def _():
                half_copy(T_ZUP + 2 * d + q, s, y, up).wait_send()

            @pl.when((z > 0) & (z + d <= 3))
            def _():
                half_copy(T_ZDOWN + 2 * d + q, s, y, down).wait_send()

            @pl.when(z - 1 - d >= 0)
            def _():
                half_copy(T_YUP + 2 * d + q, s, y, py).wait_send()

            @pl.when(z + 1 + d <= 3)
            def _():
                half_copy(T_YDOWN + 2 * d + q, s, y, py).wait_send()

    for q in range(8):
        w_copy(T_CORE + q, s, pc).wait_send()
    for u in range(6):
        core_copy(u).wait_send()
        x_copy(u).wait_send()
        for layer in z_targets(u):
            z_copy(u, layer).wait_send()


def fused(tokens, weight, cotangent):
    rows, width = tokens.shape
    shard = weight.shape[0]
    half = rows // 2
    scale = 1.0 / math.sqrt(rows * lax.axis_size("seq"))
    vmem = pl.BlockSpec(memory_space=pltpu.VMEM)
    output, d_tokens, d_weight = pl.pallas_call(
        functools.partial(kernel, scale),
        out_shape=(
            jax.ShapeDtypeStruct((rows, width), BF16),
            jax.ShapeDtypeStruct((rows, width), BF16),
            jax.ShapeDtypeStruct((shard, 3 * width), F32),
        ),
        in_specs=[vmem] * 3,
        out_specs=(vmem, vmem, vmem),
        scratch_shapes=[
            pltpu.VMEM((2, half, width), BF16),
            pltpu.VMEM((2, half, width), BF16),
            pltpu.VMEM((4 * half, width), BF16),
            pltpu.VMEM((4 * half, width), BF16),
            pltpu.VMEM((width, 3 * width), BF16),
            pltpu.VMEM((width, rows), BF16),
            pltpu.VMEM((6, 4 * shard, width), F32),
            pltpu.VMEM((6, 4 * shard, width), BF16),
            pltpu.VMEM((6, 4 * shard, width), BF16),
            pltpu.VMEM((6, 2 * shard, width), BF16),
            pltpu.VMEM((6, 2 * shard, width), BF16),
            pltpu.VMEM((3, 2 * shard, width), F32),
            pltpu.VMEM((6, 2 * shard, width), BF16),
            pltpu.VMEM((3, 3, shard, width), BF16),
            pltpu.VMEM((2, half, width), BF16),
            pltpu.VMEM((2, half, width), BF16),
            pltpu.SemaphoreType.DMA((T_COUNT,)),
            pltpu.SemaphoreType.DMA((T_COUNT,)),
        ],
        compiler_params=pltpu.CompilerParams(
            collective_id=0, has_side_effects=True, vmem_limit_bytes=52 * 1024 * 1024
        ),
        cost_estimate=pl.CostEstimate(
            flops=6 * rows * 3 * width * width, bytes_accessed=6 * rows * width * 2, transcendentals=rows * width
        ),
    )(tokens, weight.reshape(shard, 3 * width), cotangent)
    return output, d_tokens, d_weight.reshape(shard, 3, width)


def shifted(value, axis, steps):
    count = lax.axis_size(axis)
    first, last = (max(0, -steps), min(count, count - steps))
    return lax.ppermute(value, axis, [(source, source + steps) for source in range(first, last)])


def from_lower(values):
    return shifted(values, "seq", SPAN)


def received_upper(values):
    return shifted(values, "seq", -SPAN)


def general(tokens, weight, cotangent):
    rows = tokens.shape[0]
    width = tokens.shape[1]
    seq_count = lax.axis_size("seq")
    x = tokens.astype(jnp.float32)
    inv = lax.rsqrt(jnp.mean(x * x, axis=1, keepdims=True) + 1e-06)
    normalized_rows = (x * inv).astype(jnp.bfloat16)
    filter_taps = jnp.concatenate(
        [from_lower(normalized_rows), normalized_rows, received_upper(normalized_rows)], axis=1
    )
    full_weight = lax.all_gather(weight, "seq", axis=0, tiled=True)
    pre = lax.dot_general(
        filter_taps,
        full_weight.reshape(width, 3 * width),
        (((1,), (1,)), ((), ())),
        preferred_element_type=jnp.float32,
    )
    output = (x + jax.nn.gelu(pre)).astype(jnp.bfloat16)
    slope = jax.jvp(jax.nn.gelu, (pre,), (jnp.ones_like(pre),))[1]
    grad_out = cotangent.astype(jnp.float32)
    preactivation_gradient = (grad_out * slope).astype(jnp.bfloat16)
    normalized_gradient = jnp.dot(
        received_upper(preactivation_gradient),
        full_weight[:, 0, :],
        preferred_element_type=jnp.float32,
    )
    normalized_gradient = normalized_gradient + jnp.dot(
        preactivation_gradient, full_weight[:, 1, :], preferred_element_type=jnp.float32
    )
    normalized_gradient = normalized_gradient + jnp.dot(
        from_lower(preactivation_gradient), full_weight[:, 2, :], preferred_element_type=jnp.float32
    )
    inner = jnp.mean(normalized_gradient * x, axis=1, keepdims=True)
    d_tokens = (grad_out + inv * normalized_gradient - x * inv * inv * inv * inner).astype(
        jnp.bfloat16
    )
    term = lax.dot_general(
        preactivation_gradient,
        filter_taps,
        (((0,), (0,)), ((), ())),
        preferred_element_type=jnp.float32,
    )
    owned = lax.psum_scatter(term, "seq", scatter_dimension=0, tiled=True)
    scale_factor = 1.0 / jnp.sqrt(jnp.float32(rows * seq_count))
    d_weight = (owned * scale_factor).reshape(owned.shape[0], 3, width)
    return (output, d_tokens, d_weight)


def solution(mesh):
    placed = (P(("groups", "seq"), None), P("seq", None, None), P(("groups", "seq"), None))
    small = mesh.shape["groups"] == 2 and mesh.shape["seq"] == 16
    return jax.shard_map(
        fused if small else general,
        mesh=mesh,
        in_specs=placed,
        out_specs=(
            P(("groups", "seq"), None),
            P(("groups", "seq"), None),
            P(("groups", "seq"), None, None),
        ),
        check_vma=False,
    )
```
